256 devices in a mesh: year: 8 (over z), row: 8 (over x, core), col: 4 (over y).
Axes of the slice: x: 4, y: 4, z: 8, core: 2. Of those that a mesh axis runs over, the one named last changes fastest.
Arguments:
- observed: float32 [8, 46, 512, 512], P('year', None, 'row', 'col'), may hold values from 0 to 0.8
- quality: int32 [8, 46, 512, 512], P('year', None, 'row', 'col'), may hold values from 0 to 3, as said below
- land_mask: int32 [512, 512], P('row', 'col'), may hold values 0 or 1
- params: float32 [8, 7, 512, 512], P('year', None, 'row', 'col'), may hold values from -0.3 to 3.4
- spatial_weight: float32 [7], replicated, may hold values from 0.2 to 2
- temporal_weight: float32 [7], replicated, may hold values from 0.2 to 2
Outputs:
- new_params: float32 [8, 7, 512, 512], P('year', None, 'row', 'col')
- residual: float32 [8, 7, 512, 512], P('year', None, 'row', 'col')
The draws below stay inside these ranges and needn't reach their ends.
Inputs may be any that keep to these rules, and one draw needn't show every extreme that they name: `quality`: 0 good, 1 marginal, 2 snow, 3 cloud.
All inputs are finite; a program needn't handle non-finite values. No bound on the sum of `land_mask` on one device may be relied on, other than what follows from the above.
Results may differ from the reference program's by a relative error of at most 0.0003.
Values sent between devices are 32-bit elements; how exact they have to be, the bound alone decides.
No kernel may reach another device: no remote copies, remote signals or barrier semaphores. Data moves between devices by JAX's collectives and lax.ppermute only.
A program may use at most 64 MiB of HBM per device.

```python
import math
import jax
import jax.numpy as jnp
from jax import lax

DATES = 46
PARAMS = 7
ITERS = 4
YEARS = 8
NR = 512
NC = 512


def draw_quality(key, part):
    base_key = jax.random.fold_in(key, 11)
    level_key, other_key = jax.random.split(base_key)
    shape_all = (YEARS, DATES, NR, NC)
    chance = jax.random.randint(level_key, shape_all, 0, 1000)
    row_pos = lax.broadcasted_iota(jnp.int32, shape_all, 2)
    year_pos = lax.broadcasted_iota(jnp.int32, shape_all, 0)
    threshold = 250 + 600 * row_pos // max(NR - 1, 1) + 50 * year_pos // max(YEARS - 1, 1)
    others = jax.random.randint(other_key, shape_all, 1, 4)
    return jnp.where(chance < threshold, 0, others).astype(jnp.int32)


def draw_params(key, part):
    base_key = jax.random.fold_in(key, 23)
    lower = jnp.array([0.0, 0.3, -0.3, 0.25, 2.3, 0.6, 2.3], jnp.float32)
    upper = jnp.array([0.2, 0.7, 0.3, 0.45, 3.4, 0.8, 3.4], jnp.float32)
    unit = jax.random.uniform(base_key, (YEARS, PARAMS, NR, NC), jnp.float32)
    return lower[None, :, None, None] + (upper - lower)[None, :, None, None] * unit


def touch_ends(result, own_key, smallest, largest):
    longest = result.shape.index(max(result.shape))
    spots = []
    for shift in (0, 1):
        where = [jax.random.randint(jax.random.fold_in(own_key, axis), (), 0, length) for axis, length in enumerate(result.shape)]
        where[longest] = (where[longest] + shift) % result.shape[longest]
        spots.append(tuple(where))
    return result.at[spots[0]].set(smallest).at[spots[1]].set(largest)


def shard_levels(stream_key, dims, shards, low, top_value):
    loudness = 1.0
    for dim, parts in shards:
        draws = jax.random.uniform(jax.random.fold_in(jax.random.fold_in(stream_key, 6), dim), (parts,), jnp.float32, low / len(shards), top_value / len(shards))
        loudness = loudness * jnp.repeat(jnp.exp(draws), dims[dim] // parts).reshape((-1,) + (1,) * (len(dims) - 1 - dim))
    return loudness


def setup_inputs(seed: int = 0) -> dict:
    key_list = jax.random.split(jax.random.key(seed), 7)
    observed = jnp.clip(0.8 * jax.random.uniform(key_list[0], (YEARS, DATES, NR, NC), jnp.float32) ** shard_levels(key_list[0], (YEARS, DATES, NR, NC), ((0, 8), (2, 8), (3, 4)), -0.2, 0.2), 0.0, 0.8)
    quality = draw_quality(jax.random.fold_in(key_list[6], 71), 0)
    land_mask = touch_ends((jax.random.randint(key_list[2], (NR, NC), 0, 4) < 3).astype(jnp.int32), jax.random.fold_in(key_list[2], 1), 0, 1)
    params = draw_params(jax.random.fold_in(key_list[6], 71), 0)
    spatial_weight = jnp.clip(jnp.exp(jax.random.uniform(key_list[4], (PARAMS,), jnp.float32, math.log(0.2), math.log(2.0))), 0.2, 2.0)
    temporal_weight = jnp.clip(jnp.exp(jax.random.uniform(key_list[5], (PARAMS,), jnp.float32, math.log(0.2), math.log(2.0))), 0.2, 2.0)
    return {"observed": observed, "quality": quality, "land_mask": land_mask, "params": params, "spatial_weight": spatial_weight, "temporal_weight": temporal_weight}


damping = 0.1


def upper_pairs(count):
    return [(left_index, right_index) for left_index in range(count) for right_index in range(left_index, count)]


def curve_terms(observed, quality, land_mask, params):
    num_dates = observed.shape[1]
    count = params.shape[1]
    weight = jnp.where(quality == 0, 1.0, 0.0) + jnp.where(quality == 1, 0.5, 0.0)
    weight = weight * land_mask.astype(jnp.float32)[None, None] / num_dates
    date_times = (jnp.arange(num_dates, dtype=jnp.float32) / num_dates).reshape(1, num_dates, 1, 1)
    level_base, peak_value, green_slope, rise_mid, rise_log, fall_mid, fall_log = [params[:, index][:, None] for index in range(count)]
    rise_rate = jnp.exp(rise_log)
    fall_rate = jnp.exp(fall_log)
    rise_curve = jax.nn.sigmoid(rise_rate * (date_times - rise_mid))
    fall_curve = jax.nn.sigmoid(fall_rate * (date_times - fall_mid))
    season = rise_curve - fall_curve
    amplitude = peak_value - green_slope * date_times
    misfit = level_base + amplitude * season - observed
    rise_slope = rise_curve * (1.0 - rise_curve)
    fall_slope = fall_curve * (1.0 - fall_curve)
    jacobian = [jnp.ones_like(misfit), season, -date_times * season,
                -amplitude * rise_rate * rise_slope,
                amplitude * rise_slope * (date_times - rise_mid) * rise_rate,
                amplitude * fall_rate * fall_slope,
                -amplitude * fall_slope * (date_times - fall_mid) * fall_rate]
    weighted = [weight * column for column in jacobian]
    hessian = jnp.stack([jnp.sum(weighted[left_index] * jacobian[right_index], axis=1) for left_index, right_index in upper_pairs(count)])
    gradient = jnp.stack([jnp.sum(weighted[index] * misfit, axis=1) for index in range(count)], axis=1)
    return hessian, gradient


def blocks_from(hessian, count):
    blocks = [[None] * count for index in range(count)]
    for position, (left_index, right_index) in enumerate(upper_pairs(count)):
        blocks[left_index][right_index] = hessian[position]
        blocks[right_index][left_index] = hessian[position]
    return blocks


def block_apply(blocks, field):
    count = len(blocks)
    outputs = []
    for left_index in range(count):
        total = blocks[left_index][0] * field[:, 0]
        for right_index in range(1, count):
            total = total + blocks[left_index][right_index] * field[:, right_index]
        outputs.append(total)
    return jnp.stack(outputs, axis=1)


def invert(blocks):
    count = len(blocks)
    left_rows = [list(row) for row in blocks]
    right_rows = [[jnp.full_like(blocks[0][0], 1.0 if left_index == right_index else 0.0) for right_index in range(count)] for left_index in range(count)]
    for pivot in range(count):
        scale = 1.0 / left_rows[pivot][pivot]
        left_rows[pivot] = [entry * scale for entry in left_rows[pivot]]
        right_rows[pivot] = [entry * scale for entry in right_rows[pivot]]
        for other in range(count):
            if other != pivot:
                factor = left_rows[other][pivot]
                left_rows[other] = [entry - factor * base_entry for entry, base_entry in zip(left_rows[other], left_rows[pivot])]
                right_rows[other] = [entry - factor * base_entry for entry, base_entry in zip(right_rows[other], right_rows[pivot])]
    return right_rows


def prior_apply(field, spatial_weight, temporal_weight):
    padded = jnp.pad(field, ((1, 1), (0, 0), (1, 1), (1, 1)), mode="edge")
    plane = 4.0 * field - (padded[1:-1, :, :-2, 1:-1] + padded[1:-1, :, 2:, 1:-1] + padded[1:-1, :, 1:-1, :-2] + padded[1:-1, :, 1:-1, 2:])
    yearly = 2.0 * field - (padded[:-2, :, 1:-1, 1:-1] + padded[2:, :, 1:-1, 1:-1])
    return spatial_weight[None, :, None, None] * plane + temporal_weight[None, :, None, None] * yearly


def reference(observed, quality, land_mask, params, spatial_weight, temporal_weight):
    count = params.shape[1]

    def per_year(inputs):
        return curve_terms(inputs[0][None], inputs[1][None], land_mask, inputs[2][None])

    hess_all, grad_all = lax.map(per_year, (observed, quality, params))
    hessian = jnp.moveaxis(hess_all[:, :, 0], 0, 1)
    data_grad = grad_all[:, 0]
    blocks = blocks_from(hessian, count)
    shifted = [list(row) for row in blocks]
    for index in range(count):
        shifted[index][index] = blocks[index][index] + (damping + 4.0 * spatial_weight[index] + 2.0 * temporal_weight[index])
    precond = invert(shifted)

    def operate(field):
        return block_apply(blocks, field) + damping * field + prior_apply(field, spatial_weight, temporal_weight)

    residual = -(data_grad + prior_apply(params, spatial_weight, temporal_weight))
    step_field = jnp.zeros_like(params)
    search = block_apply(precond, residual)
    direction = search
    inner_now = jnp.sum(residual * search)
    for sweep in range(ITERS):
        image = operate(direction)
        step_len = inner_now / jnp.sum(direction * image)
        step_field = step_field + step_len * direction
        residual = residual - step_len * image
        if sweep + 1 < ITERS:
            search = block_apply(precond, residual)
            inner_next = jnp.sum(residual * search)
            direction = search + (inner_next / inner_now) * direction
            inner_now = inner_next
    return params + step_field, residual
```

```python
import functools

import jax
import jax.numpy as jnp
from jax import lax
from jax.experimental import pallas as pl
from jax.experimental.pallas import tpu as pltpu
from jax.sharding import PartitionSpec as P

damping = 0.1
COUNT = 7
PAIRS = [(i, j) for i in range(COUNT) for j in range(i, COUNT)]
SPOT = {}
for _n, (_i, _j) in enumerate(PAIRS):
    SPOT[_i, _j] = _n
    SPOT[_j, _i] = _n
SUB = 8
VMEM = pl.BlockSpec(memory_space=pltpu.VMEM)
SMEM = pl.BlockSpec(memory_space=pltpu.SMEM)


def blocks_kernel(num_dates, sw, tw, observed, quality, land, params, minv, grad):
    base, peak, slope, rise_mid, rise_log, fall_mid, fall_log = [params[0, k] for k in range(COUNT)]
    rise = jnp.exp(rise_log)
    fall = jnp.exp(fall_log)
    rise_half = 0.5 * rise
    fall_half = 0.5 * fall
    rise_off = rise_half * rise_mid
    fall_off = fall_half * fall_mid
    peak_half = 0.5 * peak
    slope_half = 0.5 * slope

    def date(d, sums):
        sums = list(sums)
        t = d.astype(jnp.float32) * (1.0 / num_dates)
        flag = quality[0, d]
        w = jnp.where(flag == 0, 1.0, jnp.where(flag == 1, 0.5, 0.0))
        x1 = rise_half * t - rise_off
        x2 = fall_half * t - fall_off
        th1 = jnp.tanh(x1)
        th2 = jnp.tanh(x2)
        q = th1 - th2
        m = peak_half - slope_half * t
        mis = base + m * q - observed[0, d]
        a = m - m * (th1 * th1)
        b = m - m * (th2 * th2)
        cols = [None, q, q * t, a, a * x1, b, b * x2]
        for i in range(COUNT):
            wc = w if i == 0 else w * cols[i]
            for j in range(i, COUNT):
                n = SPOT[i, j]
                sums[n] = sums[n] + (wc if j == 0 else wc * cols[j])
            sums[len(PAIRS) + i] = sums[len(PAIRS) + i] + wc * mis
        return tuple(sums)

    zero = jnp.zeros_like(base)
    sums = lax.fori_loop(0, num_dates, date, (zero,) * (len(PAIRS) + COUNT), unroll=2)
    share = land[...].astype(jnp.float32) * (1.0 / num_dates)
    scale = [None, 0.5, -0.5, -0.5 * rise, 1.0, 0.5 * fall, -1.0]
    left = [share if s is None else share * s for s in scale]
    block = {}
    for n, (i, j) in enumerate(PAIRS):
        e = sums[n] * left[i]
        if scale[j] is not None:
            e = e * scale[j]
        if i == j:
            e = e + (damping + 4.0 * sw[i] + 2.0 * tw[i])
        block[i, j] = e
    for i in range(COUNT):
        grad[i] = sums[len(PAIRS) + i] * left[i]
    key = lambda i, j: (i, j) if i <= j else (j, i)
    for k in range(COUNT):
        inv = 1.0 / block[k, k]
        row = {i: block[key(i, k)] for i in range(COUNT) if i != k}
        fac = {i: row[i] * inv for i in row}
        for i in row:
            for j in row:
                if i <= j:
                    block[i, j] = block[i, j] - fac[i] * row[j]
        for i in row:
            block[key(i, k)] = fac[i]
        block[k, k] = -inv
    for n, (i, j) in enumerate(PAIRS):
        minv[n] = -block[i, j]


def put_faces(v, row_low, row_high, col_low, col_high):
    rows, cols = v.shape[1], v.shape[2]
    lane = lax.broadcasted_iota(jnp.int32, (rows, cols), 1)
    low = jnp.zeros((rows, cols), jnp.float32)
    high = low
    for p in range(COUNT):
        row_low[p : p + 1] = v[p, 0:1]
        row_high[p : p + 1] = v[p, rows - 1 : rows]
        low = jnp.where(lane == p, v[p, :, 0:1], low)
        high = jnp.where(lane == p, v[p, :, cols - 1 : cols], high)
    row_low[COUNT : COUNT + 1] = jnp.zeros((1, cols), jnp.float32)
    row_high[COUNT : COUNT + 1] = jnp.zeros((1, cols), jnp.float32)
    col_low[...] = low
    col_high[...] = high


def faces_kernel(v, *faces):
    put_faces(v, *faces)


def low_sides(x, p, ends, ylo, rlo, clo):
    rows, cols = x.shape
    row = lax.broadcasted_iota(jnp.int32, x.shape, 0)
    lane = lax.broadcasted_iota(jnp.int32, x.shape, 1)
    yl = jnp.where(ends[0] == 1, x, ylo[p])
    face = jnp.where(ends[2] == 1, x[0:1], rlo[p : p + 1])
    rl = jnp.where(row == 0, face, pltpu.roll(x, 1, 0))
    face = jnp.where(ends[4] == 1, x[:, 0:1], clo[:, p : p + 1])
    cl = jnp.where(lane == 0, face, pltpu.roll(x, 1, 1))
    return yl, rl, cl


def high_sides(x, p, ends, yhi, rhi, chi):
    rows, cols = x.shape
    row = lax.broadcasted_iota(jnp.int32, x.shape, 0)
    lane = lax.broadcasted_iota(jnp.int32, x.shape, 1)
    yh = jnp.where(ends[1] == 1, x, yhi[p])
    face = jnp.where(ends[3] == 1, x[rows - 1 : rows], rhi[p : p + 1])
    rh = jnp.where(row == rows - 1, face, pltpu.roll(x, rows - 1, 0))
    face = jnp.where(ends[5] == 1, x[:, cols - 1 : cols], chi[:, p : p + 1])
    ch = jnp.where(lane == cols - 1, face, pltpu.roll(x, cols - 1, 1))
    return yh, rh, ch


def side_sums(x, p, ends, halo):
    ylo, rlo, clo, yhi, rhi, chi = halo
    yl, rl, cl = low_sides(x, p, ends, ylo, rlo, clo)
    yh, rh, ch = high_sides(x, p, ends, yhi, rhi, chi)
    return rl + rh + cl + ch, yl + yh


def solve_blocks(minv, u, v, dots, last=None):
    rows = u.shape[1]
    even = jnp.zeros((SUB, u.shape[2]), jnp.float32)
    odd = even
    for c in range(rows // SUB):
        at = slice(c * SUB, (c + 1) * SUB)
        us = [u[p, at] for p in range(COUNT)]
        for i in range(COUNT):
            total = minv[SPOT[i, 0], at] * us[0]
            for j in range(1, COUNT):
                total = total + minv[SPOT[i, j], at] * us[j]
            v[i, at] = total
            even = even + total * us[i]
            if last is not None:
                odd = odd + last[i, at] * us[i]
    dots[0] = even
    dots[1] = odd


def first_kernel(ends, sw, tw, minv, grad, params, *refs):
    halo, (u, v, dots), faces = refs[:6], refs[6:9], refs[9:]
    for p in range(COUNT):
        x = params[p]
        plane, yearly = side_sums(x, p, ends, halo)
        u[p] = -(grad[p] + (sw[p] * (4.0 * x - plane) + tw[p] * (2.0 * x - yearly)))
    solve_blocks(minv, u, v, dots)
    put_faces(v, *faces)


def next_kernel(ends, sw, tw, minv, last, *refs):
    halo, (u, v, dots), faces = refs[:6], refs[6:9], refs[9:]
    for p in range(COUNT):
        plane, yearly = side_sums(last[p], p, ends, halo)
        u[p] = sw[p] * plane + tw[p] * yearly
    solve_blocks(minv, u, v, dots, last)
    put_faces(v, *faces)


def moments_kernel(ends, sw, tw, v, ylo, rlo, clo, dots0, dots1, dots2, dots3, sums):
    rows, cols = v.shape[1], v.shape[2]
    row = lax.broadcasted_iota(jnp.int32, (rows, cols), 0)
    lane = lax.broadcasted_iota(jnp.int32, (rows, cols), 1)
    end = [ends[n].astype(jnp.float32) for n in range(6)]
    edge = jnp.where(row == rows - 1, end[3], 0.0) - jnp.where(row == 0, end[2], 0.0)
    edge = edge + jnp.where(lane == cols - 1, end[5], 0.0) - jnp.where(lane == 0, end[4], 0.0)
    total = jnp.zeros((rows, cols), jnp.float32)
    for p in range(COUNT):
        x = v[p]
        yl, rl, cl = low_sides(x, p, ends, ylo, rlo, clo)
        plane = 2.0 * (rl + cl) + edge * x
        yearly = 2.0 * yl + (end[1] - end[0]) * x
        total = total + x * (sw[p] * plane + tw[p] * yearly)
    last = total[0:SUB]
    for c in range(1, rows // SUB):
        last = last + total[c * SUB : (c + 1) * SUB]
    parts = [dots0[0], dots1[1], dots1[0], dots2[1], dots2[0], dots3[1], dots3[0], last]
    high = jnp.concatenate([jnp.sum(part, axis=0, keepdims=True) for part in parts], axis=0)
    high = jnp.sum(high, axis=1, keepdims=True)
    row = lax.broadcasted_iota(jnp.int32, (SUB, cols), 0)
    lane = lax.broadcasted_iota(jnp.int32, (SUB, cols), 1)
    line = jnp.sum(jnp.where(row == lane, high, 0.0), axis=0, keepdims=True)
    sums[...] = jnp.broadcast_to(line, sums.shape)


def solve4(gram, right):
    n = len(right)
    low = [[None] * n for _ in range(n)]
    diag = [None] * n
    for j in range(n):
        diag[j] = gram[j][j]
        for k in range(j):
            diag[j] = diag[j] - low[j][k] * low[j][k] * diag[k]
        for i in range(j + 1, n):
            e = gram[i][j]
            for k in range(j):
                e = e - low[i][k] * low[j][k] * diag[k]
            low[i][j] = e / diag[j]
    y = []
    for i in range(n):
        e = right[i]
        for k in range(i):
            e = e - low[i][k] * y[k]
        y.append(e)
    y = [y[i] / diag[i] for i in range(n)]
    for i in reversed(range(n)):
        for k in range(i + 1, n):
            y[i] = y[i] - low[k][i] * y[k]
    return y


def last_kernel(ends, sw, tw, sums, params, *refs):
    us, vs, halo, (new_params, residual) = refs[:4], refs[4:8], refs[8:14], refs[14:]
    rows, cols = params.shape[1], params.shape[2]
    line = jnp.sum(sums[...], axis=0, keepdims=True)
    lane = lax.broadcasted_iota(jnp.int32, line.shape, 1)
    mom = [jnp.sum(jnp.where(lane == n, line, 0.0), axis=1, keepdims=True) for n in range(8)]
    gram = [[mom[i + j] - mom[i + j + 1] for j in range(4)] for i in range(4)]
    y = [jnp.broadcast_to(e, (SUB, cols)) for e in solve4(gram, mom[:4])]
    y = [jnp.concatenate([e] * (rows // SUB), axis=0) for e in y]
    for p in range(COUNT):
        plane, yearly = side_sums(vs[3][p], p, ends, halo)
        new = sw[p] * plane + tw[p] * yearly
        step = y[0] * vs[0][p]
        for k in range(1, 4):
            step = step + y[k] * vs[k][p]
        new_params[p] = params[p] + step
        chain = [us[k][p] for k in range(4)] + [new]
        left = chain[0]
        for k in range(4):
            left = left - y[k] * (chain[k] - chain[k + 1])
        residual[p] = left


def call(kernel, out_shape, name, num_smem, args):
    return pl.pallas_call(
        kernel,
        out_shape=[jax.ShapeDtypeStruct(s, jnp.float32) for s in out_shape],
        in_specs=[SMEM] * num_smem + [VMEM] * (len(args) - num_smem),
        out_specs=[VMEM] * len(out_shape),
        compiler_params=pltpu.CompilerParams(vmem_limit_bytes=24 * 1024 * 1024),
        name=name,
    )(*args)


def ring(axis, shift):
    count = lax.axis_size(axis)
    return [(i, (i + shift) % count) for i in range(count)]


def exchange(v, faces):
    row_low, row_high, col_low, col_high = faces
    return (
        lax.ppermute(v, "year", ring("year", 1)),
        lax.ppermute(row_high, "row", ring("row", 1)),
        lax.ppermute(col_high, "col", ring("col", 1)),
        lax.ppermute(v, "year", ring("year", -1)),
        lax.ppermute(row_low, "row", ring("row", -1)),
        lax.ppermute(col_low, "col", ring("col", -1)),
    )


def per_device(observed, quality, land_mask, params, spatial_weight, temporal_weight):
    num_dates, rows, cols = observed.shape[1:]
    axes = ("year", "row", "col")
    devices = lax.axis_size(axes)
    ends = []
    for axis in axes:
        here = lax.axis_index(axis)
        ends += [here == 0, here == lax.axis_size(axis) - 1]
    ends = jnp.stack(ends).astype(jnp.int32)
    small = (ends, spatial_weight, temporal_weight)

    field = (COUNT, rows, cols)
    faces = [(SUB, cols)] * 2 + [(rows, cols)] * 2
    dots = (2, SUB, cols)
    current = params.reshape(field)
    halo = exchange(current, call(faces_kernel, faces, "faces", 0, (current,)))

    strip = lambda lead: pl.BlockSpec(lead + (SUB, cols), lambda i: (0,) * len(lead) + (i, 0))
    minv, grad = pl.pallas_call(
        functools.partial(blocks_kernel, num_dates),
        grid=(rows // SUB,),
        out_shape=[
            jax.ShapeDtypeStruct((len(PAIRS), rows, cols), jnp.float32),
            jax.ShapeDtypeStruct(field, jnp.float32),
        ],
        in_specs=[SMEM, SMEM, strip((1, num_dates)), strip((1, num_dates)), strip(()), strip((1, COUNT))],
        out_specs=[strip((len(PAIRS),)), strip((COUNT,))],
        compiler_params=pltpu.CompilerParams(vmem_limit_bytes=24 * 1024 * 1024),
        cost_estimate=pl.CostEstimate(flops=60000000, bytes_accessed=5000000, transcendentals=800000),
        name="blocks",
    )(spatial_weight, temporal_weight, observed, quality, land_mask, params)

    step_out = [field, field, dots] + faces
    u, v, dot, *face = call(
        first_kernel, step_out, "first", 3, small + (minv, grad, current) + halo
    )
    us, vs, ds = [u], [v], [dot]
    for _ in range(3):
        halo = exchange(v, face)
        u, v, dot, *face = call(next_kernel, step_out, "next", 3, small + (minv, v) + halo)
        us.append(u)
        vs.append(v)
        ds.append(dot)
    halo = exchange(v, face)
    (sums,) = call(
        moments_kernel, [(devices, cols)], "moments", 3, small + (v,) + halo[:3] + tuple(ds)
    )
    sums = lax.all_to_all(sums, axes, 0, 0, tiled=True)
    new_params, residual = call(
        last_kernel, [field, field], "last", 3, small + (sums, current) + tuple(us) + tuple(vs) + halo
    )
    return (new_params.reshape(params.shape), residual.reshape(params.shape))


def solution(mesh):
    field = P("year", None, "row", "col")
    return jax.shard_map(
        per_device,
        mesh=mesh,
        in_specs=(field, field, P("row", "col"), field, P(), P()),
        out_specs=(field, field),
        check_vma=False,
    )
```

```python
import functools

import jax
import jax.numpy as jnp
from jax import lax
from jax.experimental import pallas as pl
from jax.experimental.pallas import tpu as pltpu
from jax.sharding import PartitionSpec as P

damping = 0.1
COUNT = 7
MOMENTS = 8
PAIRS = [(i, j) for i in range(COUNT) for j in range(i, COUNT)]
SPOT = {}
for _n, (_i, _j) in enumerate(PAIRS):
    SPOT[_i, _j] = _n
    SPOT[_j, _i] = _n
SUB = 8
MIB = 1024 * 1024
VMEM = pl.BlockSpec(memory_space=pltpu.VMEM)
SMEM = pl.BlockSpec(memory_space=pltpu.SMEM)
ANY = pl.BlockSpec(memory_space=pl.ANY)
AXES = ("year", "row", "col")

SPATIAL, TEMPORAL, ENDS, ROW_EVEN, COL_EVEN, TABLE = 0, 8, 16, 19, 20, 24
GROUP = 2
START_MIB, BLOCKS_MIB = 60, 56


def strip_sums(num_dates, observed, quality, params, at):
    base, peak, slope, rise_mid, rise_log, fall_mid, fall_log = [
        params[0, k, at] for k in range(COUNT)
    ]
    rise = jnp.exp(rise_log)
    fall = jnp.exp(fall_log)
    rise_half = 0.5 * rise
    fall_half = 0.5 * fall
    rise_off = rise_half * rise_mid
    fall_off = fall_half * fall_mid
    peak_half = 0.5 * peak
    slope_half = 0.5 * slope

    def date(d, sums):
        sums = list(sums)
        t = d.astype(jnp.float32) * (1.0 / num_dates)
        flag = quality[d, at]
        w = jnp.where(flag == 0, 1.0, jnp.where(flag == 1, 0.5, 0.0))
        x1 = rise_half * t - rise_off
        x2 = fall_half * t - fall_off
        th1 = jnp.tanh(x1)
        th2 = jnp.tanh(x2)
        q = th1 - th2
        m = peak_half - slope_half * t
        mis = base + m * q - observed[d, at]
        a = m - m * (th1 * th1)
        b = m - m * (th2 * th2)
        cols = [None, q, q * t, a, a * x1, b, b * x2]
        for i in range(COUNT):
            wc = w if i == 0 else w * cols[i]
            for j in range(i, COUNT):
                n = SPOT[i, j]
                sums[n] = sums[n] + (wc if j == 0 else wc * cols[j])
            sums[len(PAIRS) + i] = sums[len(PAIRS) + i] + wc * mis
        return tuple(sums)

    zero = jnp.zeros_like(base)
    start = (zero,) * (len(PAIRS) + COUNT)
    unroll = num_dates // 2 if num_dates % 2 == 0 else 1
    return lax.fori_loop(0, num_dates, date, start, unroll=unroll), rise, fall


def invert(block):
    key = lambda i, j: (i, j) if i <= j else (j, i)
    for k in range(COUNT):
        inv = 1.0 / block[k, k]
        row = {i: block[key(i, k)] for i in range(COUNT) if i != k}
        fac = {i: row[i] * inv for i in row}
        for i in row:
            for j in row:
                if i <= j:
                    block[i, j] = block[i, j] - fac[i] * row[j]
        for i in row:
            block[key(i, k)] = fac[i]
        block[k, k] = -inv
    return block


def blocks_kernel(table, observed_far, quality_far, land, params, minv, grad, observed, quality, done):
    num_dates, rows = observed.shape[:2]
    strips = rows // SUB

    def copies(c):
        at = pl.ds(pl.multiple_of(c * SUB, SUB), SUB)
        return (
            pltpu.make_async_copy(observed_far.at[0, :, at], observed.at[:, at], done.at[0, c]),
            pltpu.make_async_copy(quality_far.at[0, :, at], quality.at[:, at], done.at[1, c]),
        )

    for c in range(strips):
        for copy in copies(c):
            copy.start()

    def strip(c, carry):
        for copy in copies(c):
            copy.wait()
        at = pl.ds(pl.multiple_of(c * SUB, SUB), SUB)
        sums, rise, fall = strip_sums(num_dates, observed, quality, params, at)
        share = land[at].astype(jnp.float32) * (1.0 / num_dates)
        scale = [None, 0.5, -0.5, -0.5 * rise, 1.0, 0.5 * fall, -1.0]
        left = [share if s is None else share * s for s in scale]
        block = {}
        for n, (i, j) in enumerate(PAIRS):
            e = sums[n] * left[i]
            if scale[j] is not None:
                e = e * scale[j]
            if i == j:
                s, t = table[SPATIAL + i : SPATIAL + i + 1], table[TEMPORAL + i : TEMPORAL + i + 1]
                e = e + (damping + 4.0 * s + 2.0 * t)
            block[i, j] = e
        for i in range(COUNT):
            grad[i, at] = sums[len(PAIRS) + i] * left[i]
        block = invert(block)
        for n, (i, j) in enumerate(PAIRS):
            minv[n, at] = -block[i, j]
        return carry

    lax.fori_loop(0, strips, strip, 0)


def flag(table, n):
    return jnp.broadcast_to(table[n : n + 1], (SUB, table.shape[1])) > 0.5


class Faces:
    def __init__(self, cols):
        shape = (SUB, cols)
        self.lane = lax.broadcasted_iota(jnp.int32, shape, 1)
        self.low = jnp.zeros(shape, jnp.float32)
        self.high = self.low

    def add(self, x, p, c):
        here = self.lane == c * SUB + p
        self.low = jnp.where(here, x[:, 0:1], self.low)
        self.high = jnp.where(here, x[:, x.shape[1] - 1 :], self.high)

    def put(self, table, v, row_a, row_b, col_a, col_b):
        rows = v.shape[1]
        even = flag(table, COL_EVEN)
        col_a[...] = jnp.where(even, self.high, self.low)
        col_b[...] = jnp.where(even, self.low, self.high)
        even = flag(table, ROW_EVEN)[0:COUNT]
        low, high = v[:, 0], v[:, rows - 1]
        zero = jnp.zeros((1, v.shape[2]), jnp.float32)
        row_a[...] = jnp.concatenate([jnp.where(even, high, low), zero], axis=0)
        row_b[...] = jnp.concatenate([jnp.where(even, low, high), zero], axis=0)


def start_kernel(ends, sw_far, tw_far, params_far, table, row_a, row_b, col_a, col_b, sw, tw, params, done):
    copies = [
        pltpu.make_async_copy(params_far, params, done.at[0]),
        pltpu.make_async_copy(sw_far, sw, done.at[1]),
        pltpu.make_async_copy(tw_far, tw, done.at[2]),
    ]
    for copy in copies:
        copy.start()
    cols = table.shape[1]
    table[...] = jnp.zeros_like(table)
    put = lambda n, value: table.__setitem__(
        slice(n, n + 1), jnp.full((1, cols), value.astype(jnp.float32), jnp.float32)
    )
    for n in range(3):
        put(ENDS + n, ends[n])
    put(ROW_EVEN, ends[3])
    put(COL_EVEN, ends[4])
    for copy in copies:
        copy.wait()
    for p in range(COUNT):
        put(SPATIAL + p, sw[p])
        put(TEMPORAL + p, tw[p])
    faces = Faces(cols)
    for c in range(params.shape[1] // SUB):
        for p in range(COUNT):
            faces.add(params[p, c * SUB : (c + 1) * SUB], p, c)
    faces.put(table, params, row_a, row_b, col_a, col_b)


class Sides:
    def __init__(self, table, v, halo):
        self.table, self.v = table, v
        self.rows, self.cols = v.shape[1], v.shape[2]
        shape = (SUB, self.cols)
        self.sub = lax.broadcasted_iota(jnp.int32, shape, 0)
        self.lane = lax.broadcasted_iota(jnp.int32, shape, 1)
        self.year_a, self.year_b, row_a, row_b, col_a, col_b = halo
        self.year_end = flag(table, ENDS)
        even, end = flag(table, ROW_EVEN)[0:COUNT], flag(table, ENDS + 1)[0:COUNT]
        a, b = row_a[0:COUNT], row_b[0:COUNT]
        self.row_low = jnp.where(even, jnp.where(end, v[:, 0], b), a)
        self.row_high = jnp.where(even, a, jnp.where(end, v[:, self.rows - 1], b))
        even, self.col_end = flag(table, COL_EVEN), flag(table, ENDS + 2)
        a, b = col_a[...], col_b[...]
        self.col_low, self.col_high = jnp.where(even, b, a), jnp.where(even, a, b)
        self.own_low = jnp.logical_and(self.col_end, even)
        self.own_high = jnp.logical_and(self.col_end, jnp.logical_not(even))
        self.edge_low = jnp.logical_and(self.lane == 0, jnp.logical_not(self.own_low))
        self.edge_high = jnp.logical_and(self.lane == self.cols - 1, jnp.logical_not(self.own_high))
        self.keep_low = jnp.logical_and(self.lane == 0, self.own_low)
        self.keep_high = jnp.logical_and(self.lane == self.cols - 1, self.own_high)

    def at(self, c):
        return slice(c * SUB, (c + 1) * SUB)

    def plane(self, x, p, c):
        if c == 0:
            face = self.row_low[p : p + 1]
        else:
            face = self.v[p, c * SUB - 1 : c * SUB]
        total = jnp.where(self.sub == 0, face, pltpu.roll(x, 1, 0))
        if (c + 1) * SUB == self.rows:
            face = self.row_high[p : p + 1]
        else:
            face = self.v[p, (c + 1) * SUB : (c + 1) * SUB + 1]
        total = total + jnp.where(self.sub == SUB - 1, face, pltpu.roll(x, SUB - 1, 0))
        n = c * SUB + p
        side = jnp.where(self.edge_low, self.col_low[:, n : n + 1], pltpu.roll(x, 1, 1))
        total = total + jnp.where(self.keep_low, x, side)
        side = jnp.where(self.edge_high, self.col_high[:, n : n + 1], pltpu.roll(x, self.cols - 1, 1))
        return total + jnp.where(self.keep_high, x, side)

    def years(self, x, p, c):
        at = self.at(c)
        return self.year_a[p, at] + jnp.where(self.year_end, x, self.year_b[p, at])

    def weights(self, p):
        return self.table[SPATIAL + p : SPATIAL + p + 1], self.table[TEMPORAL + p : TEMPORAL + p + 1]


def solve_strip(minv, at, us):
    vs = []
    for i in range(COUNT):
        total = minv[SPOT[i, 0], at] * us[0]
        for j in range(1, COUNT):
            total = total + minv[SPOT[i, j], at] * us[j]
        vs.append(total)
    return vs


def inner(total, left, right):
    for a, b in zip(left, right):
        total = total + a * b
    return total


def step_kernel(first, *refs):
    if first:
        (table, minv, grad, old), refs = refs[:4], refs[4:]
    else:
        (table, minv, old), refs = refs[:3], refs[3:]
    halo, (u, v, dots), out = refs[:6], refs[6:9], refs[9:]
    sides = Sides(table, old, halo)
    faces = Faces(old.shape[2])
    even = jnp.zeros((SUB, old.shape[2]), jnp.float32)
    odd = even
    strips = old.shape[1] // SUB
    for start in range(0, strips, GROUP):
        results = []
        for c in range(start, min(start + GROUP, strips)):
            at = sides.at(c)
            xs = [old[p, at] for p in range(COUNT)]
            us = []
            for p in range(COUNT):
                x = xs[p]
                s, t = sides.weights(p)
                plane = sides.plane(x, p, c)
                yearly = sides.years(x, p, c)
                if first:
                    us.append(-(grad[p, at] + (s * (4.0 * x - plane) + t * (2.0 * x - yearly))))
                else:
                    us.append(s * plane + t * yearly)
            vs = solve_strip(minv, at, us)
            even = inner(even, vs, us)
            if not first:
                odd = inner(odd, xs, us)
            for p in range(COUNT):
                faces.add(vs[p], p, c)
            results.append((at, us, vs))
        for at, us, vs in results:
            for p in range(COUNT):
                u[p, at] = us[p]
                v[p, at] = vs[p]
    dots[0] = even
    dots[1] = odd
    faces.put(table, v, *out)


def moments_kernel(table, v, *refs):
    halo, dots, (u, out) = refs[:6], refs[6:10], refs[10:]
    cols = v.shape[2]
    sides = Sides(table, v, halo)
    total = jnp.zeros((SUB, cols), jnp.float32)
    strips = v.shape[1] // SUB
    for start in range(0, strips, GROUP):
        results = []
        for c in range(start, min(start + GROUP, strips)):
            at = sides.at(c)
            xs = [v[p, at] for p in range(COUNT)]
            us = []
            for p in range(COUNT):
                s, t = sides.weights(p)
                us.append(s * sides.plane(xs[p], p, c) + t * sides.years(xs[p], p, c))
            total = inner(total, xs, us)
            results.append((at, us))
        for at, us in results:
            for p in range(COUNT):
                u[p, at] = us[p]
    parts = [dots[0][0], dots[1][1], dots[1][0], dots[2][1], dots[2][0], dots[3][1], dots[3][0], total]
    high = jnp.concatenate([jnp.sum(part, axis=0, keepdims=True) for part in parts], axis=0)
    high = jnp.sum(high, axis=1, keepdims=True)
    line = jnp.where(sides.lane == sides.sub, high, 0.0)
    out[...] = jnp.broadcast_to(jnp.sum(line, axis=0, keepdims=True), out.shape)


def solve4(gram, right):
    n = len(right)
    low = [[None] * n for _ in range(n)]
    diag = [None] * n
    for j in range(n):
        diag[j] = gram[j][j]
        for k in range(j):
            diag[j] = diag[j] - low[j][k] * low[j][k] * diag[k]
        for i in range(j + 1, n):
            e = gram[i][j]
            for k in range(j):
                e = e - low[i][k] * low[j][k] * diag[k]
            low[i][j] = e / diag[j]
    y = []
    for i in range(n):
        e = right[i]
        for k in range(i):
            e = e - low[i][k] * y[k]
        y.append(e)
    y = [y[i] / diag[i] for i in range(n)]
    for i in reversed(range(n)):
        for k in range(i + 1, n):
            y[i] = y[i] - low[k][i] * y[k]
    return y


def last_kernel(moments, params, *refs):
    us, vs, (new_params, residual) = refs[:5], refs[5:9], refs[9:]
    cols = params.shape[2]
    line = jnp.sum(moments[...], axis=0, keepdims=True)
    lane = lax.broadcasted_iota(jnp.int32, line.shape, 1)
    mom = [jnp.sum(jnp.where(lane == n, line, 0.0), axis=1, keepdims=True) for n in range(MOMENTS)]
    mom = [jnp.broadcast_to(e, (SUB, cols)) for e in mom]
    gram = [[mom[i + j] - mom[i + j + 1] for j in range(4)] for i in range(4)]
    y = solve4(gram, mom[:4])
    for c in range(params.shape[1] // SUB):
        at = slice(c * SUB, (c + 1) * SUB)
        results = []
        for p in range(COUNT):
            step = y[0] * vs[0][p, at]
            for k in range(1, 4):
                step = step + y[k] * vs[k][p, at]
            chain = [u[p, at] for u in us]
            left = chain[0]
            for k in range(4):
                left = left - y[k] * (chain[k] - chain[k + 1])
            results.append((params[p, at] + step, left))
        for p in range(COUNT):
            new_params[p, at], residual[p, at] = results[p]


def call(kernel, out_shape, name, args, in_specs=None, mib=24, scratch=(), cost=None):
    return pl.pallas_call(
        kernel,
        out_shape=[jax.ShapeDtypeStruct(s, jnp.float32) for s in out_shape],
        in_specs=in_specs or [VMEM] * len(args),
        out_specs=[VMEM] * len(out_shape),
        scratch_shapes=list(scratch),
        compiler_params=pltpu.CompilerParams(vmem_limit_bytes=mib * MIB),
        cost_estimate=cost,
        name=name,
    )(*args)


def pairs(axis, odd):
    count = lax.axis_size(axis)
    return [(i, ((i - odd) ^ 1) + odd if 0 <= i - odd < count - 2 * odd else count - 1 - i) for i in range(count)]


def exchange(v, faces):
    row_a, row_b, col_a, col_b = faces
    return (
        lax.ppermute(v, "year", pairs("year", 0)),
        lax.ppermute(v, "year", pairs("year", 1)),
        lax.ppermute(row_a, "row", pairs("row", 0)),
        lax.ppermute(row_b, "row", pairs("row", 1)),
        lax.ppermute(col_a, "col", pairs("col", 0)),
        lax.ppermute(col_b, "col", pairs("col", 1)),
    )


def per_device(observed, quality, land_mask, params, spatial_weight, temporal_weight):
    num_dates, rows, cols = observed.shape[1:]
    index = [lax.axis_index(axis) for axis in AXES]
    size = [lax.axis_size(axis) for axis in AXES]
    ends = [jnp.logical_or(i == 0, i == n - 1) for i, n in zip(index, size)]
    ends = jnp.stack(ends + [i % 2 == 0 for i in index[1:]]).astype(jnp.int32)

    field = (COUNT, rows, cols)
    face = (SUB, cols)
    dots = (2, SUB, cols)
    current = params.reshape(field)
    table, *faces = call(
        start_kernel,
        [(TABLE, cols)] + [face] * 4,
        "start",
        (ends, spatial_weight, temporal_weight, current),
        [SMEM, ANY, ANY, ANY],
        START_MIB,
        [
            pltpu.SMEM((COUNT,), jnp.float32),
            pltpu.SMEM((COUNT,), jnp.float32),
            pltpu.VMEM(field, jnp.float32),
            pltpu.SemaphoreType.DMA((3,)),
        ],
    )
    halo = exchange(current, faces)

    minv, grad = call(
        blocks_kernel,
        [(len(PAIRS), rows, cols), field],
        "blocks",
        (table, observed, quality, land_mask, params),
        [VMEM, ANY, ANY, VMEM, VMEM],
        BLOCKS_MIB,
        [
            pltpu.VMEM((num_dates, rows, cols), jnp.float32),
            pltpu.VMEM((num_dates, rows, cols), jnp.int32),
            pltpu.SemaphoreType.DMA((2, rows // SUB)),
        ],
        pl.CostEstimate(flops=10**10, bytes_accessed=5 * 10**6, transcendentals=10**6),
    )

    args = (table, minv, grad, current)
    us, vs, ds = [], [], []
    for k in range(4):
        u, v, dot, *faces = call(
            functools.partial(step_kernel, k == 0),
            [field, field, dots] + [face] * 4,
            "step",
            args + tuple(halo),
        )
        us.append(u)
        vs.append(v)
        ds.append(dot)
        args = (table, minv, v)
        halo = exchange(v, faces)

    devices = size[0] * size[1] * size[2]
    u, mine = call(
        moments_kernel, [field, (devices, cols)], "moments", (table, v) + tuple(halo) + tuple(ds)
    )
    moments = lax.all_to_all(mine, AXES, 0, 0, tiled=True)
    new_params, residual = call(
        last_kernel, [field, field], "last", (moments, current) + tuple(us) + (u,) + tuple(vs)
    )
    return (new_params.reshape(params.shape), residual.reshape(params.shape))


def solution(mesh):
    field = P("year", None, "row", "col")
    return jax.shard_map(
        per_device,
        mesh=mesh,
        in_specs=(field, field, P("row", "col"), field, P(), P()),
        out_specs=(field, field),
        check_vma=False,
    )
```

```python
import functools

import jax
import jax.numpy as jnp
from jax import lax
from jax.experimental import pallas as pl
from jax.experimental.pallas import tpu as pltpu
from jax.sharding import PartitionSpec as P

damping = 0.1
COUNT = 7
MOMENTS = 8
PAIRS = [(i, j) for i in range(COUNT) for j in range(i, COUNT)]
SPOT = {}
for _n, (_i, _j) in enumerate(PAIRS):
    SPOT[_i, _j] = _n
    SPOT[_j, _i] = _n
SUB = 8
KIB = 1024
VMEM = pl.BlockSpec(memory_space=pltpu.VMEM)
SMEM = pl.BlockSpec(memory_space=pltpu.SMEM)
ANY = pl.BlockSpec(memory_space=pl.ANY)
AXES = ("year", "row", "col")

SPATIAL, TEMPORAL, ENDS, ROW_EVEN, COL_EVEN, TABLE = 0, 8, 16, 19, 20, 24
GROUP = 2
START_KIB, BLOCKS_KIB = 54784, 53248


def strip_sums(num_dates, observed, quality, params, at):
    base, peak, slope, rise_mid, rise_log, fall_mid, fall_log = [
        params[k, at] for k in range(COUNT)
    ]
    rise = jnp.exp(rise_log)
    fall = jnp.exp(fall_log)
    rise_half = 0.5 * rise
    fall_half = 0.5 * fall
    rise_off = rise_half * rise_mid
    fall_off = fall_half * fall_mid
    peak_half = 0.5 * peak
    slope_half = 0.5 * slope

    def date(d, sums):
        sums = list(sums)
        t = d.astype(jnp.float32) * (1.0 / num_dates)
        flag = quality[d, at]
        w = jnp.where(flag == 0, 1.0, jnp.where(flag == 1, 0.5, 0.0))
        x1 = rise_half * t - rise_off
        x2 = fall_half * t - fall_off
        th1 = jnp.tanh(x1)
        th2 = jnp.tanh(x2)
        q = th1 - th2
        m = peak_half - slope_half * t
        mis = base + m * q - observed[d, at]
        a = m - m * (th1 * th1)
        b = m - m * (th2 * th2)
        cols = [None, q, q * t, a, a * x1, b, b * x2]
        for i in range(COUNT):
            wc = w if i == 0 else w * cols[i]
            for j in range(i, COUNT):
                n = SPOT[i, j]
                sums[n] = sums[n] + (wc if j == 0 else wc * cols[j])
            sums[len(PAIRS) + i] = sums[len(PAIRS) + i] + wc * mis
        return tuple(sums)

    zero = jnp.zeros_like(base)
    start = (zero,) * (len(PAIRS) + COUNT)
    unroll = num_dates // 2 if num_dates % 2 == 0 else 1
    return lax.fori_loop(0, num_dates, date, start, unroll=unroll), rise, fall


def invert(block):
    key = lambda i, j: (i, j) if i <= j else (j, i)
    for k in range(COUNT):
        inv = 1.0 / block[k, k]
        row = {i: block[key(i, k)] for i in range(COUNT) if i != k}
        fac = {i: row[i] * inv for i in row}
        for i in row:
            for j in row:
                if i <= j:
                    block[i, j] = block[i, j] - fac[i] * row[j]
        for i in row:
            block[key(i, k)] = fac[i]
        block[k, k] = -inv
    return block


def flag(table, n):
    return jnp.broadcast_to(table[n : n + 1], (SUB, table.shape[1])) > 0.5


class Faces:
    def __init__(self, cols):
        shape = (SUB, cols)
        self.lane = lax.broadcasted_iota(jnp.int32, shape, 1)
        self.low = jnp.zeros(shape, jnp.float32)
        self.high = self.low

    def add(self, x, p, c):
        here = self.lane == c * SUB + p
        self.low = jnp.where(here, x[:, 0:1], self.low)
        self.high = jnp.where(here, x[:, x.shape[1] - 1 :], self.high)

    def put(self, table, v, row_a, row_b, col_a, col_b):
        rows = v.shape[1]
        even = flag(table, COL_EVEN)
        col_a[...] = jnp.where(even, self.high, self.low)
        col_b[...] = jnp.where(even, self.low, self.high)
        even = flag(table, ROW_EVEN)[0:COUNT]
        low, high = v[:, 0], v[:, rows - 1]
        zero = jnp.zeros((1, v.shape[2]), jnp.float32)
        row_a[...] = jnp.concatenate([jnp.where(even, high, low), zero], axis=0)
        row_b[...] = jnp.concatenate([jnp.where(even, low, high), zero], axis=0)


def start_kernel(given, params_far, table, params, row_a, row_b, col_a, col_b, done):
    copy = pltpu.make_async_copy(params_far, params, done)
    copy.start()
    cols = table.shape[1]
    table[0:ENDS] = given[0:ENDS]
    table[ENDS:TABLE] = jnp.zeros((TABLE - ENDS, cols), jnp.float32)
    put = lambda n, value: table.__setitem__(
        slice(n, n + 1), jnp.full((1, cols), value.astype(jnp.float32), jnp.float32)
    )
    index = [lax.axis_index(axis) for axis in AXES]
    for n, axis in enumerate(AXES):
        put(ENDS + n, jnp.logical_or(index[n] == 0, index[n] == lax.axis_size(axis) - 1).astype(jnp.int32))
    put(ROW_EVEN, 1 - lax.rem(index[1], 2))
    put(COL_EVEN, 1 - lax.rem(index[2], 2))
    copy.wait()
    faces = Faces(cols)
    for c in range(params.shape[1] // SUB):
        for p in range(COUNT):
            faces.add(params[p, c * SUB : (c + 1) * SUB], p, c)
    faces.put(table, params, row_a, row_b, col_a, col_b)


def blocks_kernel(table, given, params, observed_far, quality_far, minv, grad, observed, quality, done):
    num_dates, rows, cols = observed.shape
    strips = rows // SUB

    def copies(c):
        at = pl.ds(pl.multiple_of(c * SUB, SUB), SUB)
        return (
            pltpu.make_async_copy(observed_far.at[0, :, at], observed.at[:, at], done.at[0, c]),
            pltpu.make_async_copy(quality_far.at[0, :, at], quality.at[:, at], done.at[1, c]),
        )

    for c in range(strips):
        for copy in copies(c):
            copy.start()

    def strip(c, carry):
        for copy in copies(c):
            copy.wait()
        at = pl.ds(pl.multiple_of(c * SUB, SUB), SUB)
        sums, rise, fall = strip_sums(num_dates, observed, quality, params, at)
        share = given[pl.ds(pl.multiple_of(ENDS + c * SUB, SUB), SUB)] * (1.0 / num_dates)
        scale = [None, 0.5, -0.5, -0.5 * rise, 1.0, 0.5 * fall, -1.0]
        left = [share if s is None else share * s for s in scale]
        block = {}
        for n, (i, j) in enumerate(PAIRS):
            e = sums[n] * left[i]
            if scale[j] is not None:
                e = e * scale[j]
            if i == j:
                s, t = table[SPATIAL + i : SPATIAL + i + 1], table[TEMPORAL + i : TEMPORAL + i + 1]
                e = e + (damping + 4.0 * s + 2.0 * t)
            block[i, j] = e
        for i in range(COUNT):
            grad[i, at] = sums[len(PAIRS) + i] * left[i]
        block = invert(block)
        for n, (i, j) in enumerate(PAIRS):
            minv[n, at] = -block[i, j]
        return carry

    lax.fori_loop(0, strips, strip, 0)


class Sides:
    def __init__(self, table, v, halo):
        self.table, self.v = table, v
        self.rows, self.cols = v.shape[1], v.shape[2]
        shape = (SUB, self.cols)
        self.sub = lax.broadcasted_iota(jnp.int32, shape, 0)
        self.lane = lax.broadcasted_iota(jnp.int32, shape, 1)
        self.year_a, self.year_b, row_a, row_b, col_a, col_b = halo
        self.year_end = flag(table, ENDS)
        even, end = flag(table, ROW_EVEN)[0:COUNT], flag(table, ENDS + 1)[0:COUNT]
        a, b = row_a[0:COUNT], row_b[0:COUNT]
        self.row_low = jnp.where(even, jnp.where(end, v[:, 0], b), a)
        self.row_high = jnp.where(even, a, jnp.where(end, v[:, self.rows - 1], b))
        even, self.col_end = flag(table, COL_EVEN), flag(table, ENDS + 2)
        a, b = col_a[...], col_b[...]
        self.col_low, self.col_high = jnp.where(even, b, a), jnp.where(even, a, b)
        self.own_low = jnp.logical_and(self.col_end, even)
        self.own_high = jnp.logical_and(self.col_end, jnp.logical_not(even))
        self.edge_low = jnp.logical_and(self.lane == 0, jnp.logical_not(self.own_low))
        self.edge_high = jnp.logical_and(self.lane == self.cols - 1, jnp.logical_not(self.own_high))
        self.keep_low = jnp.logical_and(self.lane == 0, self.own_low)
        self.keep_high = jnp.logical_and(self.lane == self.cols - 1, self.own_high)

    def at(self, c):
        return slice(c * SUB, (c + 1) * SUB)

    def plane(self, x, p, c):
        if c == 0:
            face = self.row_low[p : p + 1]
        else:
            face = self.v[p, c * SUB - 1 : c * SUB]
        total = jnp.where(self.sub == 0, face, pltpu.roll(x, 1, 0))
        if (c + 1) * SUB == self.rows:
            face = self.row_high[p : p + 1]
        else:
            face = self.v[p, (c + 1) * SUB : (c + 1) * SUB + 1]
        total = total + jnp.where(self.sub == SUB - 1, face, pltpu.roll(x, SUB - 1, 0))
        n = c * SUB + p
        side = jnp.where(self.edge_low, self.col_low[:, n : n + 1], pltpu.roll(x, 1, 1))
        total = total + jnp.where(self.keep_low, x, side)
        side = jnp.where(self.edge_high, self.col_high[:, n : n + 1], pltpu.roll(x, self.cols - 1, 1))
        return total + jnp.where(self.keep_high, x, side)

    def years(self, x, p, c):
        at = self.at(c)
        return self.year_a[p, at] + jnp.where(self.year_end, x, self.year_b[p, at])

    def weights(self, p):
        return self.table[SPATIAL + p : SPATIAL + p + 1], self.table[TEMPORAL + p : TEMPORAL + p + 1]


def solve_strip(minv, at, us):
    vs = []
    for i in range(COUNT):
        total = minv[SPOT[i, 0], at] * us[0]
        for j in range(1, COUNT):
            total = total + minv[SPOT[i, j], at] * us[j]
        vs.append(total)
    return vs


def inner(total, left, right):
    for a, b in zip(left, right):
        total = total + a * b
    return total


def step_kernel(first, *refs):
    if first:
        (table, minv, grad, old), refs = refs[:4], refs[4:]
    else:
        (table, minv, old), refs = refs[:3], refs[3:]
    halo, (u, v, dots), out = refs[:6], refs[6:9], refs[9:]
    sides = Sides(table, old, halo)
    faces = Faces(old.shape[2])
    even = jnp.zeros((SUB, old.shape[2]), jnp.float32)
    odd = even
    strips = old.shape[1] // SUB
    for start in range(0, strips, GROUP):
        results = []
        for c in range(start, min(start + GROUP, strips)):
            at = sides.at(c)
            xs = [old[p, at] for p in range(COUNT)]
            us = []
            for p in range(COUNT):
                x = xs[p]
                s, t = sides.weights(p)
                plane = sides.plane(x, p, c)
                yearly = sides.years(x, p, c)
                if first:
                    us.append(-(grad[p, at] + (s * (4.0 * x - plane) + t * (2.0 * x - yearly))))
                else:
                    us.append(s * plane + t * yearly)
            vs = solve_strip(minv, at, us)
            even = inner(even, vs, us)
            if not first:
                odd = inner(odd, xs, us)
            for p in range(COUNT):
                faces.add(vs[p], p, c)
            results.append((at, us, vs))
        for at, us, vs in results:
            for p in range(COUNT):
                u[p, at] = us[p]
                v[p, at] = vs[p]
    dots[0] = even
    dots[1] = odd
    faces.put(table, v, *out)


def moments_kernel(table, v, *refs):
    halo, dots, (u, out) = refs[:6], refs[6:10], refs[10:]
    cols = v.shape[2]
    sides = Sides(table, v, halo)
    total = jnp.zeros((SUB, cols), jnp.float32)
    strips = v.shape[1] // SUB
    for start in range(0, strips, GROUP):
        results = []
        for c in range(start, min(start + GROUP, strips)):
            at = sides.at(c)
            xs = [v[p, at] for p in range(COUNT)]
            us = []
            for p in range(COUNT):
                s, t = sides.weights(p)
                us.append(s * sides.plane(xs[p], p, c) + t * sides.years(xs[p], p, c))
            total = inner(total, xs, us)
            results.append((at, us))
        for at, us in results:
            for p in range(COUNT):
                u[p, at] = us[p]
    parts = [dots[0][0], dots[1][1], dots[1][0], dots[2][1], dots[2][0], dots[3][1], dots[3][0], total]
    high = jnp.concatenate([jnp.sum(part, axis=0, keepdims=True) for part in parts], axis=0)
    high = jnp.sum(high, axis=1, keepdims=True)
    line = jnp.where(sides.lane == sides.sub, high, 0.0)
    out[...] = jnp.broadcast_to(jnp.sum(line, axis=0, keepdims=True), out.shape)


def solve4(gram, right):
    n = len(right)
    low = [[None] * n for _ in range(n)]
    diag = [None] * n
    for j in range(n):
        diag[j] = gram[j][j]
        for k in range(j):
            diag[j] = diag[j] - low[j][k] * low[j][k] * diag[k]
        for i in range(j + 1, n):
            e = gram[i][j]
            for k in range(j):
                e = e - low[i][k] * low[j][k] * diag[k]
            low[i][j] = e / diag[j]
    y = []
    for i in range(n):
        e = right[i]
        for k in range(i):
            e = e - low[i][k] * y[k]
        y.append(e)
    y = [y[i] / diag[i] for i in range(n)]
    for i in reversed(range(n)):
        for k in range(i + 1, n):
            y[i] = y[i] - low[k][i] * y[k]
    return y


def last_kernel(moments, params, *refs):
    us, vs, (new_params, residual) = refs[:5], refs[5:9], refs[9:]
    cols = params.shape[2]
    line = jnp.sum(moments[...], axis=0, keepdims=True)
    lane = lax.broadcasted_iota(jnp.int32, line.shape, 1)
    mom = [jnp.sum(jnp.where(lane == n, line, 0.0), axis=1, keepdims=True) for n in range(MOMENTS)]
    mom = [jnp.broadcast_to(e, (SUB, cols)) for e in mom]
    gram = [[mom[i + j] - mom[i + j + 1] for j in range(4)] for i in range(4)]
    y = solve4(gram, mom[:4])
    for c in range(params.shape[1] // SUB):
        at = slice(c * SUB, (c + 1) * SUB)
        results = []
        for p in range(COUNT):
            step = y[0] * vs[0][p, at]
            for k in range(1, 4):
                step = step + y[k] * vs[k][p, at]
            chain = [u[p, at] for u in us]
            left = chain[0]
            for k in range(4):
                left = left - y[k] * (chain[k] - chain[k + 1])
            results.append((params[p, at] + step, left))
        for p in range(COUNT):
            new_params[p, at], residual[p, at] = results[p]


def call(kernel, out_shape, name, args, in_specs=None, kib=24576, scratch=(), cost=None):
    return pl.pallas_call(
        kernel,
        out_shape=[jax.ShapeDtypeStruct(s, jnp.float32) for s in out_shape],
        in_specs=in_specs or [VMEM] * len(args),
        out_specs=[VMEM] * len(out_shape),
        scratch_shapes=list(scratch),
        compiler_params=pltpu.CompilerParams(vmem_limit_bytes=kib * KIB),
        cost_estimate=cost,
        name=name,
    )(*args)


def pairs(axis, odd):
    count = lax.axis_size(axis)
    return [(i, ((i - odd) ^ 1) + odd if 0 <= i - odd < count - 2 * odd else count - 1 - i) for i in range(count)]


def exchange(v, faces):
    row_a, row_b, col_a, col_b = faces
    return (
        lax.ppermute(v, "year", pairs("year", 0)),
        lax.ppermute(v, "year", pairs("year", 1)),
        lax.ppermute(row_a, "row", pairs("row", 0)),
        lax.ppermute(row_b, "row", pairs("row", 1)),
        lax.ppermute(col_a, "col", pairs("col", 0)),
        lax.ppermute(col_b, "col", pairs("col", 1)),
    )


def per_device(observed, quality, land_mask, params, spatial_weight, temporal_weight):
    num_dates, rows, cols = observed.shape[1:]
    field = (COUNT, rows, cols)
    face = (SUB, cols)
    dots = (2, SUB, cols)
    far = params.reshape(field)
    spread = lambda w: jnp.pad(jnp.broadcast_to(w[:, None], (COUNT, cols)), ((0, SUB - COUNT), (0, 0)))
    given = jnp.concatenate(
        [spread(spatial_weight), spread(temporal_weight), land_mask.astype(jnp.float32)]
    )
    table, current, *faces = call(
        start_kernel,
        [(TABLE, cols), field] + [face] * 4,
        "start",
        (given, far),
        [VMEM, ANY],
        START_KIB,
        [pltpu.SemaphoreType.DMA],
    )
    halo = exchange(far, faces)
    minv, grad = call(
        blocks_kernel,
        [(len(PAIRS), rows, cols), field],
        "blocks",
        (table, given, current, observed, quality),
        [VMEM, VMEM, VMEM, ANY, ANY],
        BLOCKS_KIB,
        [
            pltpu.VMEM((num_dates, rows, cols), jnp.float32),
            pltpu.VMEM((num_dates, rows, cols), jnp.int32),
            pltpu.SemaphoreType.DMA((2, rows // SUB)),
        ],
        pl.CostEstimate(flops=10**10, bytes_accessed=5 * 10**6, transcendentals=10**6),
    )

    args = (table, minv, grad, current)
    us, vs, ds = [], [], []
    for k in range(4):
        u, v, dot, *faces = call(
            functools.partial(step_kernel, k == 0),
            [field, field, dots] + [face] * 4,
            "step",
            args + tuple(halo),
        )
        us.append(u)
        vs.append(v)
        ds.append(dot)
        args = (table, minv, v)
        halo = exchange(v, faces)

    devices = lax.axis_size(AXES)
    u, mine = call(
        moments_kernel, [field, (devices, cols)], "moments", (table, v) + tuple(halo) + tuple(ds)
    )
    moments = lax.all_to_all(mine, AXES, 0, 0, tiled=True)
    new_params, residual = call(
        last_kernel, [field, field], "last", (moments, current) + tuple(us) + (u,) + tuple(vs)
    )
    return (new_params.reshape(params.shape), residual.reshape(params.shape))


def solution(mesh):
    field = P("year", None, "row", "col")
    return jax.shard_map(
        per_device,
        mesh=mesh,
        in_specs=(field, field, P("row", "col"), field, P(), P()),
        out_specs=(field, field),
        check_vma=False,
    )
```

```python
import functools

import jax
import jax.numpy as jnp
from jax import lax
from jax.experimental import pallas as pl
from jax.experimental.pallas import tpu as pltpu
from jax.sharding import PartitionSpec as P

ITERS = 4
damping = 0.1
COUNT = 7
MOMENTS = 8
PAIRS = [(i, j) for i in range(COUNT) for j in range(i, COUNT)]
SPOT = {}
for _n, (_i, _j) in enumerate(PAIRS):
    SPOT[_i, _j] = _n
    SPOT[_j, _i] = _n
SUB = 8
KIB = 1024
VMEM = pl.BlockSpec(memory_space=pltpu.VMEM)
SMEM = pl.BlockSpec(memory_space=pltpu.SMEM)
ANY = pl.BlockSpec(memory_space=pl.ANY)
AXES = ("year", "row", "col")

SPATIAL, TEMPORAL, ENDS, ROW_EVEN, COL_EVEN, TABLE = 0, 8, 16, 19, 20, 24
GROUP = 2
SMALLEST = 0.01
START_KIB, BLOCKS_KIB = 54784, 53248


def strip_sums(num_dates, observed, quality, params, at):
    base, peak, slope, rise_mid, rise_log, fall_mid, fall_log = [
        params[k, at] for k in range(COUNT)
    ]
    rise = jnp.exp(rise_log)
    fall = jnp.exp(fall_log)
    rise_half = 0.5 * rise
    fall_half = 0.5 * fall
    rise_off = rise_half * rise_mid
    fall_off = fall_half * fall_mid
    peak_half = 0.5 * peak
    slope_half = 0.5 * slope

    def date(d, sums):
        sums = list(sums)
        t = d.astype(jnp.float32) * (1.0 / num_dates)
        flag = quality[d, at]
        w = jnp.where(flag == 0, 1.0, jnp.where(flag == 1, 0.5, 0.0))
        x1 = rise_half * t - rise_off
        x2 = fall_half * t - fall_off
        th1 = jnp.tanh(x1)
        th2 = jnp.tanh(x2)
        q = th1 - th2
        m = peak_half - slope_half * t
        mis = base + m * q - observed[d, at]
        a = m - m * (th1 * th1)
        b = m - m * (th2 * th2)
        cols = [None, q, q * t, a, a * x1, b, b * x2]
        for i in range(COUNT):
            wc = w if i == 0 else w * cols[i]
            for j in range(i, COUNT):
                n = SPOT[i, j]
                sums[n] = sums[n] + (wc if j == 0 else wc * cols[j])
            sums[len(PAIRS) + i] = sums[len(PAIRS) + i] + wc * mis
        return tuple(sums)

    zero = jnp.zeros_like(base)
    start = (zero,) * (len(PAIRS) + COUNT)
    unroll = num_dates // 2 if num_dates % 2 == 0 else 1
    return lax.fori_loop(0, num_dates, date, start, unroll=unroll), rise, fall


def invert(block):
    key = lambda i, j: (i, j) if i <= j else (j, i)
    for k in range(COUNT):
        inv = 1.0 / block[k, k]
        row = {i: block[key(i, k)] for i in range(COUNT) if i != k}
        fac = {i: row[i] * inv for i in row}
        for i in row:
            for j in row:
                if i <= j:
                    block[i, j] = block[i, j] - fac[i] * row[j]
        for i in row:
            block[key(i, k)] = fac[i]
        block[k, k] = -inv
    return block


def flag(table, n):
    return jnp.broadcast_to(table[n : n + 1], (SUB, table.shape[1])) > 0.5


class Faces:
    def __init__(self, cols):
        shape = (SUB, cols)
        self.lane = lax.broadcasted_iota(jnp.int32, shape, 1)
        self.low = jnp.zeros(shape, jnp.float32)
        self.high = self.low

    def add(self, x, p, c):
        here = self.lane == c * SUB + p
        self.low = jnp.where(here, x[:, 0:1], self.low)
        self.high = jnp.where(here, x[:, x.shape[1] - 1 :], self.high)

    def put(self, table, v, row_a, row_b, col_a, col_b):
        rows = v.shape[1]
        even = flag(table, COL_EVEN)
        col_a[...] = jnp.where(even, self.high, self.low)
        col_b[...] = jnp.where(even, self.low, self.high)
        even = flag(table, ROW_EVEN)[0:COUNT]
        low, high = v[:, 0], v[:, rows - 1]
        zero = jnp.zeros((1, v.shape[2]), jnp.float32)
        row_a[...] = jnp.concatenate([jnp.where(even, high, low), zero], axis=0)
        row_b[...] = jnp.concatenate([jnp.where(even, low, high), zero], axis=0)


def start_kernel(given, params_far, table, params, row_a, row_b, col_a, col_b, done):
    copy = pltpu.make_async_copy(params_far, params, done)
    copy.start()
    cols = table.shape[1]
    table[0:ENDS] = given[0:ENDS]
    table[ENDS:TABLE] = jnp.zeros((TABLE - ENDS, cols), jnp.float32)
    put = lambda n, value: table.__setitem__(
        slice(n, n + 1), jnp.full((1, cols), value.astype(jnp.float32), jnp.float32)
    )
    index = [lax.axis_index(axis) for axis in AXES]
    for n, axis in enumerate(AXES):
        put(ENDS + n, jnp.logical_or(index[n] == 0, index[n] == lax.axis_size(axis) - 1).astype(jnp.int32))
    put(ROW_EVEN, 1 - lax.rem(index[1], 2))
    put(COL_EVEN, 1 - lax.rem(index[2], 2))
    copy.wait()
    faces = Faces(cols)
    for c in range(params.shape[1] // SUB):
        for p in range(COUNT):
            faces.add(params[p, c * SUB : (c + 1) * SUB], p, c)
    faces.put(table, params, row_a, row_b, col_a, col_b)


def blocks_kernel(table, given, params, observed_far, quality_far, minv, grad, observed, quality, done):
    num_dates, rows, cols = observed.shape
    strips = rows // SUB

    def copies(c):
        at = pl.ds(pl.multiple_of(c * SUB, SUB), SUB)
        return (
            pltpu.make_async_copy(observed_far.at[0, :, at], observed.at[:, at], done.at[0, c]),
            pltpu.make_async_copy(quality_far.at[0, :, at], quality.at[:, at], done.at[1, c]),
        )

    for c in range(strips):
        for copy in copies(c):
            copy.start()

    def strip(c, carry):
        for copy in copies(c):
            copy.wait()
        at = pl.ds(pl.multiple_of(c * SUB, SUB), SUB)
        sums, rise, fall = strip_sums(num_dates, observed, quality, params, at)
        share = given[pl.ds(pl.multiple_of(ENDS + c * SUB, SUB), SUB)] * (1.0 / num_dates)
        scale = [None, 0.5, -0.5, -0.5 * rise, 1.0, 0.5 * fall, -1.0]
        left = [share if s is None else share * s for s in scale]
        block = {}
        for n, (i, j) in enumerate(PAIRS):
            e = sums[n] * left[i]
            if scale[j] is not None:
                e = e * scale[j]
            if i == j:
                s, t = table[SPATIAL + i : SPATIAL + i + 1], table[TEMPORAL + i : TEMPORAL + i + 1]
                e = e + (damping + 4.0 * s + 2.0 * t)
            block[i, j] = e
        for i in range(COUNT):
            grad[i, at] = sums[len(PAIRS) + i] * left[i]
        block = invert(block)
        for n, (i, j) in enumerate(PAIRS):
            minv[n, at] = -block[i, j]
        return carry

    lax.fori_loop(0, strips, strip, 0)


class Sides:
    def __init__(self, table, v, halo):
        self.table, self.v = table, v
        self.rows, self.cols = v.shape[1], v.shape[2]
        shape = (SUB, self.cols)
        self.sub = lax.broadcasted_iota(jnp.int32, shape, 0)
        self.lane = lax.broadcasted_iota(jnp.int32, shape, 1)
        self.year_a, self.year_b, row_a, row_b, col_a, col_b = halo
        self.year_end = flag(table, ENDS)
        even, end = flag(table, ROW_EVEN)[0:COUNT], flag(table, ENDS + 1)[0:COUNT]
        a, b = row_a[0:COUNT], row_b[0:COUNT]
        self.row_low = jnp.where(even, jnp.where(end, v[:, 0], b), a)
        self.row_high = jnp.where(even, a, jnp.where(end, v[:, self.rows - 1], b))
        even, self.col_end = flag(table, COL_EVEN), flag(table, ENDS + 2)
        a, b = col_a[...], col_b[...]
        self.col_low, self.col_high = jnp.where(even, b, a), jnp.where(even, a, b)
        self.own_low = jnp.logical_and(self.col_end, even)
        self.own_high = jnp.logical_and(self.col_end, jnp.logical_not(even))
        self.edge_low = jnp.logical_and(self.lane == 0, jnp.logical_not(self.own_low))
        self.edge_high = jnp.logical_and(self.lane == self.cols - 1, jnp.logical_not(self.own_high))
        self.keep_low = jnp.logical_and(self.lane == 0, self.own_low)
        self.keep_high = jnp.logical_and(self.lane == self.cols - 1, self.own_high)

    def at(self, c):
        return slice(c * SUB, (c + 1) * SUB)

    def plane(self, x, p, c):
        if c == 0:
            face = self.row_low[p : p + 1]
        else:
            face = self.v[p, c * SUB - 1 : c * SUB]
        total = jnp.where(self.sub == 0, face, pltpu.roll(x, 1, 0))
        if (c + 1) * SUB == self.rows:
            face = self.row_high[p : p + 1]
        else:
            face = self.v[p, (c + 1) * SUB : (c + 1) * SUB + 1]
        total = total + jnp.where(self.sub == SUB - 1, face, pltpu.roll(x, SUB - 1, 0))
        n = c * SUB + p
        side = jnp.where(self.edge_low, self.col_low[:, n : n + 1], pltpu.roll(x, 1, 1))
        total = total + jnp.where(self.keep_low, x, side)
        side = jnp.where(self.edge_high, self.col_high[:, n : n + 1], pltpu.roll(x, self.cols - 1, 1))
        return total + jnp.where(self.keep_high, x, side)

    def years(self, x, p, c):
        at = self.at(c)
        return self.year_a[p, at] + jnp.where(self.year_end, x, self.year_b[p, at])

    def weights(self, p):
        return self.table[SPATIAL + p : SPATIAL + p + 1], self.table[TEMPORAL + p : TEMPORAL + p + 1]


def solve_strip(minv, at, us):
    vs = []
    for i in range(COUNT):
        total = minv[SPOT[i, 0], at] * us[0]
        for j in range(1, COUNT):
            total = total + minv[SPOT[i, j], at] * us[j]
        vs.append(total)
    return vs


def inner(total, left, right):
    for a, b in zip(left, right):
        total = total + a * b
    return total


def step_kernel(first, *refs):
    if first:
        (table, minv, grad, old), refs = refs[:4], refs[4:]
    else:
        (table, minv, old), refs = refs[:3], refs[3:]
    halo, (u, v, dots), out = refs[:6], refs[6:9], refs[9:]
    sides = Sides(table, old, halo)
    faces = Faces(old.shape[2])
    even = jnp.zeros((SUB, old.shape[2]), jnp.float32)
    odd = even
    strips = old.shape[1] // SUB
    for start in range(0, strips, GROUP):
        results = []
        for c in range(start, min(start + GROUP, strips)):
            at = sides.at(c)
            xs = [old[p, at] for p in range(COUNT)]
            us = []
            for p in range(COUNT):
                x = xs[p]
                s, t = sides.weights(p)
                plane = sides.plane(x, p, c)
                yearly = sides.years(x, p, c)
                if first:
                    us.append(-(grad[p, at] + (s * (4.0 * x - plane) + t * (2.0 * x - yearly))))
                else:
                    us.append(s * plane + t * yearly)
            vs = solve_strip(minv, at, us)
            even = inner(even, vs, us)
            if not first:
                odd = inner(odd, xs, us)
            for p in range(COUNT):
                faces.add(vs[p], p, c)
            results.append((at, us, vs))
        for at, us, vs in results:
            for p in range(COUNT):
                u[p, at] = us[p]
                v[p, at] = vs[p]
    dots[0] = even
    dots[1] = odd
    faces.put(table, v, *out)


def moments_kernel(table, v, *refs):
    halo, dots, (u, out) = refs[:6], refs[6:10], refs[10:]
    cols = v.shape[2]
    sides = Sides(table, v, halo)
    total = jnp.zeros((SUB, cols), jnp.float32)
    strips = v.shape[1] // SUB
    for start in range(0, strips, GROUP):
        results = []
        for c in range(start, min(start + GROUP, strips)):
            at = sides.at(c)
            xs = [v[p, at] for p in range(COUNT)]
            us = []
            for p in range(COUNT):
                s, t = sides.weights(p)
                us.append(s * sides.plane(xs[p], p, c) + t * sides.years(xs[p], p, c))
            total = inner(total, xs, us)
            results.append((at, us))
        for at, us in results:
            for p in range(COUNT):
                u[p, at] = us[p]
    parts = [dots[0][0], dots[1][1], dots[1][0], dots[2][1], dots[2][0], dots[3][1], dots[3][0], total]
    high = jnp.concatenate([jnp.sum(part, axis=0, keepdims=True) for part in parts], axis=0)
    high = jnp.sum(high, axis=1, keepdims=True)
    line = jnp.where(sides.lane == sides.sub, high, 0.0)
    out[...] = jnp.broadcast_to(jnp.sum(line, axis=0, keepdims=True), out.shape)


def solve4(gram, right):
    n = len(right)
    low = [[None] * n for _ in range(n)]
    diag = [None] * n
    for j in range(n):
        diag[j] = gram[j][j]
        for k in range(j):
            diag[j] = diag[j] - low[j][k] * low[j][k] * diag[k]
        for i in range(j + 1, n):
            e = gram[i][j]
            for k in range(j):
                e = e - low[i][k] * low[j][k] * diag[k]
            low[i][j] = e / diag[j]
    y = []
    for i in range(n):
        e = right[i]
        for k in range(i):
            e = e - low[i][k] * y[k]
        y.append(e)
    y = [y[i] / diag[i] for i in range(n)]
    for i in reversed(range(n)):
        for k in range(i + 1, n):
            y[i] = y[i] - low[k][i] * y[k]
    return y, [d / gram[n][n] for n, d in enumerate(diag)]


def last_kernel(moments, params, *refs):
    us, vs, (new_params, residual, again) = refs[:5], refs[5:9], refs[9:]
    cols = params.shape[2]
    line = jnp.sum(moments[...], axis=0, keepdims=True)
    lane = lax.broadcasted_iota(jnp.int32, line.shape, 1)
    mom = [jnp.sum(jnp.where(lane == n, line, 0.0), axis=1, keepdims=True) for n in range(MOMENTS)]
    mom = [jnp.broadcast_to(e, (SUB, cols)) for e in mom]
    gram = [[mom[i + j] - mom[i + j + 1] for j in range(4)] for i in range(4)]
    y, parts = solve4(gram, mom[:4])
    fine = functools.reduce(jnp.minimum, parts) >= SMALLEST
    again[0] = jnp.max(jnp.where(fine, 0, 1))
    for c in range(params.shape[1] // SUB):
        at = slice(c * SUB, (c + 1) * SUB)
        results = []
        for p in range(COUNT):
            step = y[0] * vs[0][p, at]
            for k in range(1, 4):
                step = step + y[k] * vs[k][p, at]
            chain = [u[p, at] for u in us]
            left = chain[0]
            for k in range(4):
                left = left - y[k] * (chain[k] - chain[k + 1])
            results.append((params[p, at] + step, left))
        for p in range(COUNT):
            new_params[p, at], residual[p, at] = results[p]


def call(kernel, out_shape, name, args, in_specs=None, kib=24576, scratch=(), cost=None):
    return pl.pallas_call(
        kernel,
        out_shape=[jax.ShapeDtypeStruct(s, jnp.float32) for s in out_shape],
        in_specs=in_specs or [VMEM] * len(args),
        out_specs=[VMEM] * len(out_shape),
        scratch_shapes=list(scratch),
        compiler_params=pltpu.CompilerParams(vmem_limit_bytes=kib * KIB),
        cost_estimate=cost,
        name=name,
    )(*args)


def pairs(axis, odd):
    count = lax.axis_size(axis)
    return [(i, ((i - odd) ^ 1) + odd if 0 <= i - odd < count - 2 * odd else count - 1 - i) for i in range(count)]


def exchange(v, faces):
    row_a, row_b, col_a, col_b = faces
    return (
        lax.ppermute(v, "year", pairs("year", 0)),
        lax.ppermute(v, "year", pairs("year", 1)),
        lax.ppermute(row_a, "row", pairs("row", 0)),
        lax.ppermute(row_b, "row", pairs("row", 1)),
        lax.ppermute(col_a, "col", pairs("col", 0)),
        lax.ppermute(col_b, "col", pairs("col", 1)),
    )


def with_halo(cells, sides, width):
    for axis, dim in sides:
        count = lax.axis_size(axis)
        ends = count - 1
        head = lax.slice_in_dim(cells, 0, width, axis=dim)
        tail = lax.slice_in_dim(cells, cells.shape[dim] - width, cells.shape[dim], axis=dim)
        cells = jnp.concatenate(
            [
                lax.ppermute(tail, axis, [(i, (i + 1) % count) for i in range(ends)]),
                cells,
                lax.ppermute(head, axis, [((i + 1) % count, i) for i in range(ends)]),
            ],
            axis=dim,
        )
    return cells


def upper_pairs(count):
    return [
        (left_index, right_index)
        for left_index in range(count)
        for right_index in range(left_index, count)
    ]


def curve_terms(observed, quality, land_mask, params):
    num_dates = observed.shape[1]
    count = params.shape[1]
    weight = jnp.where(quality == 0, 1.0, 0.0) + jnp.where(quality == 1, 0.5, 0.0)
    weight = weight * land_mask.astype(jnp.float32)[None, None] / num_dates
    date_times = (jnp.arange(num_dates, dtype=jnp.float32) / num_dates).reshape(1, num_dates, 1, 1)
    level_base, peak_value, green_slope, rise_mid, rise_log, fall_mid, fall_log = [
        params[:, index][:, None] for index in range(count)
    ]
    rise_rate = jnp.exp(rise_log)
    fall_rate = jnp.exp(fall_log)
    rise_curve = jax.nn.sigmoid(rise_rate * (date_times - rise_mid))
    fall_curve = jax.nn.sigmoid(fall_rate * (date_times - fall_mid))
    season = rise_curve - fall_curve
    amplitude = peak_value - green_slope * date_times
    misfit = level_base + amplitude * season - observed
    rise_slope = rise_curve * (1.0 - rise_curve)
    fall_slope = fall_curve * (1.0 - fall_curve)
    jacobian = [
        jnp.ones_like(misfit),
        season,
        -date_times * season,
        -amplitude * rise_rate * rise_slope,
        amplitude * rise_slope * (date_times - rise_mid) * rise_rate,
        amplitude * fall_rate * fall_slope,
        -amplitude * fall_slope * (date_times - fall_mid) * fall_rate,
    ]
    weighted = [weight * column for column in jacobian]
    hessian = jnp.stack(
        [
            jnp.sum(weighted[left_index] * jacobian[right_index], axis=1)
            for left_index, right_index in upper_pairs(count)
        ]
    )
    gradient = jnp.stack(
        [jnp.sum(weighted[index] * misfit, axis=1) for index in range(count)], axis=1
    )
    return (hessian, gradient)


def blocks_from(hessian, count):
    blocks = [[None] * count for index in range(count)]
    for position, (left_index, right_index) in enumerate(upper_pairs(count)):
        blocks[left_index][right_index] = hessian[position]
        blocks[right_index][left_index] = hessian[position]
    return blocks


def block_apply(blocks, field):
    count = len(blocks)
    outputs = []
    for left_index in range(count):
        total = blocks[left_index][0] * field[:, 0]
        for right_index in range(1, count):
            total = total + blocks[left_index][right_index] * field[:, right_index]
        outputs.append(total)
    return jnp.stack(outputs, axis=1)


def invert_blocks(blocks):
    count = len(blocks)
    left_rows = [list(row) for row in blocks]
    right_rows = [
        [
            jnp.full_like(blocks[0][0], 1.0 if left_index == right_index else 0.0)
            for right_index in range(count)
        ]
        for left_index in range(count)
    ]
    for pivot in range(count):
        scale = 1.0 / left_rows[pivot][pivot]
        left_rows[pivot] = [entry * scale for entry in left_rows[pivot]]
        right_rows[pivot] = [entry * scale for entry in right_rows[pivot]]
        for other in range(count):
            if other != pivot:
                factor = left_rows[other][pivot]
                left_rows[other] = [
                    entry - factor * base_entry
                    for entry, base_entry in zip(left_rows[other], left_rows[pivot])
                ]
                right_rows[other] = [
                    entry - factor * base_entry
                    for entry, base_entry in zip(right_rows[other], right_rows[pivot])
                ]
    return right_rows


def prior_apply(field, spatial_weight, temporal_weight):
    num_years = field.shape[0]
    num_rows = field.shape[2]
    num_cols = field.shape[3]
    padded = with_halo(field, (("year", 0), ("row", 2), ("col", 3)), 1)
    year_pad = padded[:, :, 1:-1, 1:-1]
    plane_pad = padded[1:-1]
    year_pos = (
        lax.broadcasted_iota(jnp.int32, (num_years, 1, 1, 1), 0)
        + lax.axis_index("year") * num_years
    )
    row_pos = (
        lax.broadcasted_iota(jnp.int32, (1, 1, num_rows, 1), 2) + lax.axis_index("row") * num_rows
    )
    col_pos = (
        lax.broadcasted_iota(jnp.int32, (1, 1, 1, num_cols), 3) + lax.axis_index("col") * num_cols
    )
    year_low = jnp.where(year_pos == 0, field, year_pad[:-2])
    year_high = jnp.where(year_pos == num_years * lax.axis_size("year") - 1, field, year_pad[2:])
    row_low = jnp.where(row_pos == 0, field, plane_pad[:, :, :-2, 1:-1])
    row_high = jnp.where(
        row_pos == num_rows * lax.axis_size("row") - 1, field, plane_pad[:, :, 2:, 1:-1]
    )
    col_low = jnp.where(col_pos == 0, field, plane_pad[:, :, 1:-1, :-2])
    col_high = jnp.where(
        col_pos == num_cols * lax.axis_size("col") - 1, field, plane_pad[:, :, 1:-1, 2:]
    )
    plane = 4.0 * field - (row_low + row_high + col_low + col_high)
    yearly = 2.0 * field - (year_low + year_high)
    return (
        spatial_weight[None, :, None, None] * plane + temporal_weight[None, :, None, None] * yearly
    )


def inner_total(left_field, right_field):
    return lax.psum(jnp.sum(left_field * right_field), ("year", "row", "col"))


def plain_steps(observed, quality, land_mask, params, spatial_weight, temporal_weight):
    count = params.shape[1]
    hessian, data_grad = curve_terms(observed, quality, land_mask, params)
    blocks = blocks_from(hessian, count)
    shifted = [list(row) for row in blocks]
    for index in range(count):
        shifted[index][index] = blocks[index][index] + (
            damping + 4.0 * spatial_weight[index] + 2.0 * temporal_weight[index]
        )
    precond = invert_blocks(shifted)
    residual = -(data_grad + prior_apply(params, spatial_weight, temporal_weight))
    step_field = jnp.zeros_like(params)
    search = block_apply(precond, residual)
    direction = search
    inner_now = inner_total(residual, search)
    for sweep in range(ITERS):
        image = (
            block_apply(blocks, direction)
            + damping * direction
            + prior_apply(direction, spatial_weight, temporal_weight)
        )
        step_len = inner_now / lax.psum(jnp.sum(direction * image), ("year", "row", "col"))
        step_field = step_field + step_len * direction
        residual = residual - step_len * image
        if sweep + 1 < ITERS:
            search = block_apply(precond, residual)
            inner_next = inner_total(residual, search)
            direction = search + inner_next / inner_now * direction
            inner_now = inner_next
    return (params + step_field, residual)


def per_device(observed, quality, land_mask, params, spatial_weight, temporal_weight):
    num_dates, rows, cols = observed.shape[1:]
    field = (COUNT, rows, cols)
    face = (SUB, cols)
    dots = (2, SUB, cols)
    far = params.reshape(field)
    place = lambda x, top: lax.pad(
        x.astype(jnp.float32), 0.0, ((top, ENDS + rows - top - x.shape[0], 0), (0, 0, 0))
    )
    spread = lambda w: jnp.broadcast_to(w[:, None], (COUNT, cols))
    given = place(spread(spatial_weight), SPATIAL) + place(spread(temporal_weight), TEMPORAL)
    given = given + place(land_mask, ENDS)
    table, current, *faces = call(
        start_kernel,
        [(TABLE, cols), field] + [face] * 4,
        "start",
        (given, far),
        [VMEM, ANY],
        START_KIB,
        [pltpu.SemaphoreType.DMA],
    )
    halo = exchange(far, faces)
    minv, grad = call(
        blocks_kernel,
        [(len(PAIRS), rows, cols), field],
        "blocks",
        (table, given, current, observed, quality),
        [VMEM, VMEM, VMEM, ANY, ANY],
        BLOCKS_KIB,
        [
            pltpu.VMEM((num_dates, rows, cols), jnp.float32),
            pltpu.VMEM((num_dates, rows, cols), jnp.int32),
            pltpu.SemaphoreType.DMA((2, rows // SUB)),
        ],
        pl.CostEstimate(flops=10**10, bytes_accessed=5 * 10**6, transcendentals=10**6),
    )

    args = (table, minv, grad, current)
    us, vs, ds = [], [], []
    for k in range(4):
        u, v, dot, *faces = call(
            functools.partial(step_kernel, k == 0),
            [field, field, dots] + [face] * 4,
            "step",
            args + tuple(halo),
        )
        us.append(u)
        vs.append(v)
        ds.append(dot)
        args = (table, minv, v)
        halo = exchange(v, faces)

    devices = lax.axis_size(AXES)
    u, mine = call(
        moments_kernel, [field, (devices, cols)], "moments", (table, v) + tuple(halo) + tuple(ds)
    )
    moments = lax.all_to_all(mine, AXES, 0, 0, tiled=True)
    new_params, residual, again = pl.pallas_call(
        last_kernel,
        out_shape=[jax.ShapeDtypeStruct(field, jnp.float32)] * 2 + [jax.ShapeDtypeStruct((1,), jnp.int32)],
        in_specs=[VMEM] * 11,
        out_specs=[VMEM, VMEM, SMEM],
        compiler_params=pltpu.CompilerParams(vmem_limit_bytes=24 * 1024 * KIB),
        name="last",
    )(moments, current, *us, u, *vs)

    def once_more(carry):
        given = (observed, quality, land_mask, params, spatial_weight, temporal_weight)
        given = lax.optimization_barrier(given + carry[:2])[:6]
        return plain_steps(*given) + (jnp.int32(0),)

    carry = (new_params.reshape(params.shape), residual.reshape(params.shape), again.reshape(()))
    return lax.while_loop(lambda carry: carry[2] > 0, once_more, carry)[:2]


def solution(mesh):
    field = P("year", None, "row", "col")
    return jax.shard_map(
        per_device,
        mesh=mesh,
        in_specs=(field, field, P("row", "col"), field, P(), P()),
        out_specs=(field, field),
        check_vma=False,
    )
```
